256 devices in a mesh: sub: 128 (over x, z_hi, y, core), rng: 2 (over z_lo).
Axes of the slice: x: 4, y: 4, z: 8 (z_hi: 4, z_lo: 2; z = z_hi * 2 + z_lo), core: 2. Of those that a mesh axis runs over, the one named last changes fastest.
Arguments:
- image: float32 [2, 16384, 2048], P(None, 'sub', 'rng'), may hold values from -6 to 6
- angle_offset: int32 [4, 2, 128], P(None, None, 'sub'), may hold values from -2 to 2
- angle_fraction: float32 [4, 2, 16384], P(None, None, 'sub'), may hold values from -0.5 to 0.5
- integer_distance_shifts: int32 [4, 2, 128], P(None, None, 'sub'), may hold values from -59 to 59
- subcell_distance_shares: float32 [4, 2, 16384], P(None, None, 'sub'), may hold values from -0.5 to 0.5
Outputs:
- merged: float32 [2, 16384, 2048], P(None, 'sub', 'rng')
The draws below stay inside these ranges and needn't reach their ends.
All inputs are finite; a program needn't handle non-finite values.
Results may differ from the reference program's by a relative error of at most 0.0003.
Values sent between devices are 32-bit elements; how exact they have to be, the bound alone decides.
A program may use at most 64 MiB of HBM per device.

```python
import jax
import jax.numpy as jnp
from jax import lax

A = 128
TILE = 128
HALO = 64
LEVELS = 4
NSUB = 128
RANGE = 2048


def place_ends(drawn, stream_key, smallest, high):
    place = [jax.random.randint(jax.random.fold_in(stream_key, axis), (), 0, length) for axis, length in enumerate(drawn.shape)]
    longest = drawn.shape.index(max(drawn.shape))
    beside = place[:longest] + [(place[longest] + 1) % drawn.shape[longest]] + place[longest + 1:]
    return drawn.at[tuple(place)].set(smallest).at[tuple(beside)].set(high)


def shard_levels(key, shape, cuts, least, top_value):
    level = 1.0
    for dim, parts in cuts:
        steps = jax.random.uniform(jax.random.fold_in(jax.random.fold_in(key, 6), dim), (parts,), jnp.float32, least / len(cuts), top_value / len(cuts))
        level = level * jnp.repeat(jnp.exp(steps), shape[dim] // parts).reshape((-1,) + (1,) * (len(shape) - 1 - dim))
    return level


def centred(rng, shape, scale, reach, pieces=(), dtype=jnp.bfloat16):
    factor_of = shard_levels(rng, shape, pieces, -0.22, 0.18) if pieces else 1.0
    entries = jax.random.normal(rng, shape, jnp.float32) * scale * factor_of
    return jnp.minimum(jnp.maximum(entries, -reach), reach).astype(dtype)


def setup_inputs(seed: int = 0) -> dict:
    key_list = jax.random.split(jax.random.key(seed), 6)
    image = centred(key_list[0], (2, NSUB * A, RANGE), 1.0, 6.0, ((1, 128), (2, 2)), jnp.float32)
    angle_offset = place_ends(jax.random.randint(key_list[1], (LEVELS, 2, NSUB * A // TILE), -2, 3), jax.random.fold_in(key_list[1], 1), -2, 2).astype(jnp.int32)
    angle_fraction = jnp.clip(jax.random.uniform(key_list[2], (LEVELS, 2, NSUB * A), jnp.float32, -0.5, 0.5) * shard_levels(key_list[2], (LEVELS, 2, NSUB * A), ((2, 128),), -0.4, 0.0), -0.5, 0.5)
    integer_distance_shifts = place_ends(jax.random.randint(key_list[3], (LEVELS, 2, NSUB * A // TILE), 5 - HALO, HALO - 4), jax.random.fold_in(key_list[3], 1), 5 - HALO, (HALO - 4) - 1).astype(jnp.int32)
    subcell_distance_shares = jnp.clip(jax.random.uniform(key_list[4], (LEVELS, 2, NSUB * A), jnp.float32, -0.5, 0.5) * shard_levels(key_list[4], (LEVELS, 2, NSUB * A), ((2, 128),), -0.4, 0.0), -0.5, 0.5)
    return dict(image=image, angle_offset=angle_offset, angle_fraction=angle_fraction, integer_distance_shifts=integer_distance_shifts, subcell_distance_shares=subcell_distance_shares)


frequency_quotient = 3.7


def keys_kernel(sample_displacement):
    magnitude = jnp.abs(sample_displacement)
    inner_part = (1.5 * magnitude - 2.5) * magnitude * magnitude + 1.0
    outer_part = ((-0.5 * magnitude + 2.5) * magnitude - 4.0) * magnitude + 2.0
    return jnp.where(magnitude < 1.0, inner_part, jnp.where(magnitude < 2.0, outer_part, 0.0))


def sinc_taper(sample_displacement):
    window = 0.54 + 0.46 * jnp.cos(jnp.pi * sample_displacement / 4.0)
    return jnp.where(jnp.abs(sample_displacement) < 4.0, jnp.sinc(sample_displacement) * window, 0.0)


def range_shift(tile_block, sample_displacement, fraction):
    output_breadth = tile_block.shape[-1] - 2 * HALO
    start = (HALO - 4 + sample_displacement).astype(jnp.int32)
    window = lax.dynamic_slice_in_dim(tile_block, start, output_breadth + 8, 2)
    summed = jnp.zeros(tile_block.shape[:2] + (output_breadth,), jnp.float32)
    for shift_tap in range(9):
        weight = sinc_taper(shift_tap - 4 - fraction)
        summed = summed + weight[None, :, None] * window[:, :, shift_tap:shift_tap + output_breadth]
    return summed


def child_term(child, upper_half, angle_offset, angle_fraction, integer_distance_shifts, subcell_distance_shares):
    beam_count = child.shape[1]
    tile_count = angle_offset.shape[0]
    parent_group_span = beam_count // tile_count
    parent = jnp.arange(beam_count).astype(jnp.float32)
    column = jnp.arange(beam_count).astype(jnp.float32)
    position = 0.5 * (upper_half.astype(jnp.float32) * beam_count + parent)
    position = position + jnp.repeat(angle_offset, parent_group_span).astype(jnp.float32) + angle_fraction
    weights = keys_kernel(column[None, :] - position[:, None])
    steered = jnp.einsum("ij,pjr->pir", weights, child, precision=lax.Precision.HIGHEST)
    image_groups = steered.reshape(2, tile_count, parent_group_span, steered.shape[-1])
    shifted = jax.vmap(range_shift, in_axes=(1, 0, 0), out_axes=1)(
        image_groups, integer_distance_shifts, subcell_distance_shares.reshape(tile_count, parent_group_span))
    shifted = shifted.reshape(2, beam_count, shifted.shape[-1])
    viewing_bearing = frequency_quotient * jnp.pi * (jnp.repeat(integer_distance_shifts, parent_group_span).astype(jnp.float32) + subcell_distance_shares)
    cosine = jnp.cos(viewing_bearing)[:, None]
    sine_part = jnp.sin(viewing_bearing)[:, None]
    return jnp.stack([cosine * shifted[0] - sine_part * shifted[1], sine_part * shifted[0] + cosine * shifted[1]])


def merge_pair(children, upper_half, angle_offset, angle_fraction, integer_distance_shifts, subcell_distance_shares):
    summed = None
    for which in range(2):
        rotated = child_term(children[which], upper_half, angle_offset[which], angle_fraction[which],
                             integer_distance_shifts[which], subcell_distance_shares[which])
        summed = rotated if summed is None else summed + rotated
    return summed * 0.70710678


def reference(image, angle_offset, angle_fraction, integer_distance_shifts, subcell_distance_shares):
    slot_count = image.shape[1] // A
    samples = image.shape[2]
    current = image.reshape(2, slot_count, A, samples)
    for level in range(LEVELS):
        bit_value = 1 << level
        sub_index = jnp.arange(slot_count)
        low_index = sub_index - jnp.bitwise_and(sub_index, bit_value)
        upper_half = jnp.bitwise_and(jnp.right_shift(sub_index, level), 1).astype(jnp.int32)
        padded = jnp.pad(current, ((0, 0), (0, 0), (0, 0), (HALO, HALO)))
        child_low = padded[:, low_index]
        child_high = padded[:, low_index + bit_value]
        offsets_angle = angle_offset[level].reshape(2, slot_count, -1)
        fractions_angle = angle_fraction[level].reshape(2, slot_count, A)
        offsets_range = integer_distance_shifts[level].reshape(2, slot_count, -1)
        range_fraction_table = subcell_distance_shares[level].reshape(2, slot_count, A)
        current = jax.vmap(merge_pair, in_axes=((1, 1), 0, 1, 1, 1, 1), out_axes=1)(
            (child_low, child_high), upper_half, offsets_angle, fractions_angle, offsets_range, range_fraction_table)
    return current.reshape(2, slot_count * A, samples)
```

```python
import math

import jax
import jax.numpy as jnp
from jax import lax
from jax.experimental import pallas as pl
from jax.experimental.pallas import tpu as pltpu
from jax.sharding import PartitionSpec as P

LEVELS = 4
BEAMS = 128
HALF = 64
EDGE = 64
CHUNK = 128
GROUP = 8
PACKED = CHUNK + GROUP
LAG = (1, 3, 5, 8)
MESH = pl.DeviceIdType.MESH
F32, BF16 = jnp.float32, jnp.bfloat16


def keys_kernel(distance):
    m = jnp.abs(distance)
    inner = (1.5 * m - 2.5) * m * m + 1.0
    outer = ((-0.5 * m + 2.5) * m - 4.0) * m + 2.0
    return jnp.where(m < 1.0, inner, jnp.where(m < 2.0, outer, 0.0))


def split(x):
    high = x.astype(BF16)
    return high, (x - high.astype(F32)).astype(BF16)


def kernel(samples, angle_ref, shift_ref, image_ref, fraction_ref, share_ref, out_ref, cur, sent, got, own_halo,
           partner_halo, steered, w_high, w_low, rows8, taps, send_sem, recv_sem, halo_send, halo_recv):
    chunks = samples // CHUNK
    sub, rng = lax.axis_index("sub"), lax.axis_index("rng")
    ups = [lax.rem(sub // (1 << level), 2) for level in range(LEVELS)]
    partners = [sub + (1 - 2 * up) * (1 << level) for level, up in enumerate(ups)]
    other = 1 - rng

    barrier = pltpu.get_barrier_semaphore()
    neighbours = [(sub, other)] + [(p, r) for p in partners for r in (rng, other)]
    for device in neighbours:
        pl.semaphore_signal(barrier, inc=1, device_id=device, device_id_type=MESH)

    def start_row(c):
        return pl.multiple_of(jnp.where(rng == 1, c * CHUNK, samples - (c + 1) * CHUNK), CHUNK)

    for level in range(LEVELS):
        for role in range(2):
            child = ups[level] if role == 0 else 1 - ups[level]
            row = 2 * level + role
            share = share_ref[level, pl.ds(child, 1), :]
            whole = lax.rem(37 * (shift_ref[level, child, 0] + 60), 20)
            rows8[0, row : row + 1, :] = share
            rows8[1, row : row + 1, :] = whole.astype(F32) * 0.05 + 1.85 * share
    share = rows8[0]
    turns = rows8[1]
    angle = (2.0 * math.pi) * (turns - jnp.round(turns))
    rows8[2] = jnp.cos(angle) * 0.70710678
    rows8[3] = jnp.sin(angle) * 0.70710678
    sine = jnp.sin(math.pi * share)
    cosine4 = jnp.cos((math.pi / 4) * share)
    sine4 = jnp.sin((math.pi / 4) * share)
    for k in range(-4, 5):
        x = k - share
        window = 0.54 + 0.46 * (math.cos(math.pi * k / 4) * cosine4 + math.sin(math.pi * k / 4) * sine4)
        signed = sine if k % 2 else -sine
        near = x == 0.0
        sinc = jnp.where(near, 1.0, signed / (math.pi * jnp.where(near, 1.0, x)))
        taps[k + 4] = jnp.where(jnp.abs(x) < 4.0, sinc * window, 0.0)

    lane = lax.broadcasted_iota(jnp.int32, (1, BEAMS), 1)
    row128 = lax.broadcasted_iota(jnp.int32, (BEAMS, BEAMS), 0)
    row8 = lax.broadcasted_iota(jnp.int32, (GROUP, BEAMS), 0)

    def weights(level):
        up = ups[level]
        for role in range(2):
            child = up if role == 0 else 1 - up
            row = 2 * level + role
            position = 0.5 * (up * BEAMS + lane).astype(F32)
            position = position + angle_ref[level, child, 0].astype(F32) + fraction_ref[level, pl.ds(child, 1), :]
            cos, sin = rows8[2, row : row + 1, :], rows8[3, row : row + 1, :]
            if role == 0:
                keys = keys_kernel(row128.astype(F32) - position)
                top = jnp.concatenate([keys * cos, keys * sin], axis=1)
                bottom = jnp.concatenate([keys * -sin, keys * cos], axis=1)
            else:
                keys = keys_kernel((row128[:HALF] + HALF * up).astype(F32) - position)
                top = jnp.concatenate(
                    [jnp.concatenate([keys * cos, keys * sin], axis=1),
                     jnp.concatenate([keys * -sin, keys * cos], axis=1)], axis=0)
                beam = HALF - 4 * up + lax.rem(row8, 4)
                keys = keys_kernel(beam.astype(F32) - position)
                real = row8 < 4
                eight = jnp.concatenate(
                    [keys * jnp.where(real, cos, -sin), keys * jnp.where(real, sin, cos)], axis=1)
                bottom = jnp.concatenate([eight] * (BEAMS // GROUP), axis=0)
            for part, block in enumerate((top, bottom)):
                high, low = split(block)
                w_high[level, role, part * BEAMS : (part + 1) * BEAMS, :] = high
                w_low[level, role, part * BEAMS : (part + 1) * BEAMS, :] = low

    for level in range(LEVELS):
        weights(level)

    outside = pl.multiple_of(jnp.where(rng == 1, samples + EDGE, 0), EDGE)
    for level in range(LEVELS):
        for role in range(2):
            for plane in range(2):
                steered[level, role, plane, pl.ds(outside, EDGE), :] = jnp.zeros((EDGE, BEAMS), F32)

    pl.semaphore_wait(barrier, len(neighbours))

    def partner_copy(level, c):
        return pltpu.make_async_remote_copy(
            src_ref=sent.at[level, c], dst_ref=got.at[level, c], send_sem=send_sem.at[level, c],
            recv_sem=recv_sem.at[level, c], device_id=(partners[level], rng), device_id_type=MESH)

    def halo_copies(level):
        first = pl.multiple_of(jnp.where(rng == 1, 0, samples - EDGE), EDGE)
        piece = pl.multiple_of(jnp.where(rng == 1, 0, HALF), GROUP)
        return (
            pltpu.make_async_remote_copy(
                src_ref=cur.at[level, :, pl.ds(first, EDGE), :], dst_ref=own_halo.at[level],
                send_sem=halo_send.at[level, 0], recv_sem=halo_recv.at[level, 0],
                device_id=(sub, other), device_id_type=MESH),
            pltpu.make_async_remote_copy(
                src_ref=sent.at[level, 0, pl.ds(piece, EDGE + GROUP), :], dst_ref=partner_halo.at[level],
                send_sem=halo_send.at[level, 1], recv_sem=halo_recv.at[level, 1],
                device_id=(partners[level], other), device_id_type=MESH))

    def steer(level, role, x, row):
        high, low = split(x)
        wh, wl = w_high[level, role], w_low[level, role]
        s = jnp.dot(high, wh, preferred_element_type=F32)
        s = s + jnp.dot(low, wh, preferred_element_type=F32)
        s = s + jnp.dot(high, wl, preferred_element_type=F32)
        for plane in range(2):
            steered[level, role, plane, pl.ds(row, x.shape[0]), :] = s[:, plane * BEAMS : (plane + 1) * BEAMS]

    def unpack(main, margins, first_group):
        blocks = []
        for g in range(main.shape[0] // GROUP):
            blocks.append(jnp.where(lane // GROUP == first_group + g, margins, 0.0))
        return jnp.concatenate([main, jnp.concatenate(blocks, axis=0)], axis=1)

    def produce(level, c):
        row = start_row(c)
        up = ups[level]
        theirs = 1 - up
        near = cur[level, theirs, pl.ds(row, CHUNK), :]
        far = pltpu.roll(cur[level, up, pl.ds(row, CHUNK), :], HALF, 1)
        main = jnp.where((lane < HALF) == (theirs == 0), near, far)
        first = HALF - 4 * theirs
        real = cur[level, 0, pl.ds(row, CHUNK), :]
        imag = cur[level, 1, pl.ds(row, CHUNK), :]
        both = jnp.where((lane >= first) & (lane < first + 4), real, pltpu.roll(imag, 4, 1))
        margins = jnp.zeros((GROUP, BEAMS), F32)
        for g in range(CHUNK // GROUP):
            turned = pltpu.roll(both[g * GROUP : (g + 1) * GROUP], lax.rem(g * GROUP - first + BEAMS, BEAMS), 1)
            margins = jnp.where(lane // GROUP == g, turned, margins)
        sent[level, c, 0:HALF, :] = main[:HALF]
        sent[level, c, HALF : HALF + GROUP, :] = margins
        sent[level, c, HALF + GROUP : PACKED, :] = main[HALF:]
        partner_copy(level, c).start()

        @pl.when(c == 0)
        def _():
            for copy in halo_copies(level):
                copy.start()

        steer(level, 0, jnp.concatenate([real, imag], axis=1), row + EDGE)

    def steer_halo(level):
        for copy in halo_copies(level):
            copy.wait_recv()
        row = pl.multiple_of(jnp.where(rng == 1, 0, samples + EDGE), EDGE)
        steer(level, 0, jnp.concatenate([own_halo[level, 0], own_halo[level, 1]], axis=1), row)
        main = partner_halo[level, pl.ds(pl.multiple_of(rng * GROUP, GROUP), EDGE), :]
        margins = partner_halo[level, pl.ds(pl.multiple_of((1 - rng) * EDGE, GROUP), GROUP), :]
        steer(level, 1, unpack(main, margins, rng * GROUP), row)

    def merge(level, c):
        row = start_row(c)
        shifts = [shift_ref[level, ups[level] if role == 0 else 1 - ups[level], 0] for role in range(2)]
        for plane in range(2):
            total = None
            for role in range(2):
                for k in range(9):
                    weight = taps[k, 2 * level + role : 2 * level + role + 1, :]
                    term = weight * steered[level, role, plane, pl.ds(row + (EDGE - 4 + k) + shifts[role], CHUNK), :]
                    total = term if total is None else total + term
            if level + 1 < LEVELS:
                cur[level + 1, plane, pl.ds(row, CHUNK), :] = total
            else:
                out_ref[plane, :, pl.ds(row, CHUNK)] = total.T
        if level + 1 < LEVELS:
            produce(level + 1, c)

    def consume(level, c):
        @pl.when(c < chunks)
        def _():
            partner_copy(level, c).wait_recv()
            block = got[level, c]
            main = jnp.concatenate([block[:HALF], block[HALF + GROUP :]], axis=0)
            steer(level, 1, unpack(main, block[HALF : HALF + GROUP], 0), start_row(c) + EDGE)

        @pl.when(c == 0)
        def _():
            steer_halo(level)

        @pl.when(c > 0)
        def _():
            merge(level, c - 1)

    def step(k, carry):
        @pl.when(k < chunks)
        def _():
            row = start_row(k)
            for plane in range(2):
                cur[0, plane, pl.ds(row, CHUNK), :] = image_ref[plane, :, pl.ds(row, CHUNK)].T
            produce(0, k)

        for level in range(LEVELS):
            c = k - LAG[level]

            @pl.when((c >= 0) & (c <= chunks))
            def _():
                consume(level, c)

        return carry

    lax.fori_loop(0, chunks + LAG[-1] + 1, step, 0)

    def finish(c, carry):
        for level in range(LEVELS):
            partner_copy(level, c).wait_send()
        return carry

    lax.fori_loop(0, chunks, finish, 0)
    for level in range(LEVELS):
        for copy in halo_copies(level):
            copy.wait_send()


def per_device(image, angle_offset, angle_fraction, integer_distance_shifts, subcell_distance_shares):
    samples = image.shape[2]
    chunks = samples // CHUNK
    vmem, smem = pl.BlockSpec(memory_space=pltpu.VMEM), pl.BlockSpec(memory_space=pltpu.SMEM)
    return pl.pallas_call(
        lambda *refs: kernel(samples, *refs),
        out_shape=jax.ShapeDtypeStruct(image.shape, F32),
        in_specs=[smem, smem, vmem, vmem, vmem],
        out_specs=vmem,
        scratch_shapes=[
            pltpu.VMEM((LEVELS, 2, samples, BEAMS), F32),
            pltpu.VMEM((LEVELS, chunks, PACKED, BEAMS), F32),
            pltpu.VMEM((LEVELS, chunks, PACKED, BEAMS), F32),
            pltpu.VMEM((LEVELS, 2, EDGE, BEAMS), F32),
            pltpu.VMEM((LEVELS, EDGE + GROUP, BEAMS), F32),
            pltpu.VMEM((LEVELS, 2, 2, samples + 2 * EDGE, BEAMS), F32),
            pltpu.VMEM((LEVELS, 2, 2 * BEAMS, 2 * BEAMS), BF16),
            pltpu.VMEM((LEVELS, 2, 2 * BEAMS, 2 * BEAMS), BF16),
            pltpu.VMEM((4, 2 * LEVELS, BEAMS), F32),
            pltpu.VMEM((9, 2 * LEVELS, BEAMS), F32),
            pltpu.SemaphoreType.DMA((LEVELS, chunks)),
            pltpu.SemaphoreType.DMA((LEVELS, chunks)),
            pltpu.SemaphoreType.DMA((LEVELS, 2)),
            pltpu.SemaphoreType.DMA((LEVELS, 2)),
        ],
        compiler_params=pltpu.CompilerParams(
            collective_id=0, has_side_effects=True, vmem_limit_bytes=48 * 1024 * 1024),
    )(angle_offset, integer_distance_shifts, image, angle_fraction, subcell_distance_shares)


def solution(mesh):
    placed = (P(None, "sub", "rng"),) + (P(None, None, "sub"),) * 4
    return jax.shard_map(
        per_device, mesh=mesh, in_specs=placed, out_specs=P(None, "sub", "rng"), check_vma=False)
```

```python
import math

import jax
import jax.numpy as jnp
from jax import lax
from jax.experimental import pallas as pl
from jax.experimental.pallas import tpu as pltpu
from jax.sharding import PartitionSpec as P

LEVELS = 4
BEAMS = 128
HALF = 64
EDGE = 64
CHUNK = 128
GROUP = 8
PACKED = CHUNK + GROUP
AHEAD = 2
LAG = (2, 4, 7, 10)
ORDER = (-1, 0, 1, 2, 3)
MESH = pl.DeviceIdType.MESH
F32, BF16 = jnp.float32, jnp.bfloat16


def keys_kernel(distance):
    m = jnp.abs(distance)
    inner = (1.5 * m - 2.5) * m * m + 1.0
    outer = ((-0.5 * m + 2.5) * m - 4.0) * m + 2.0
    return jnp.where(m < 1.0, inner, jnp.where(m < 2.0, outer, 0.0))


def split(x):
    high = x.astype(BF16)
    return high, (x - high.astype(F32)).astype(BF16)


def kernel(samples, angle_ref, shift_ref, image_ref, fraction_ref, share_ref, out_ref, image, cur, sent, got, own_halo,
           partner_halo, steered, weight, rows8, taps, image_sem, send_sem, recv_sem, halo_send, halo_recv):
    chunks = samples // CHUNK
    sub, rng = lax.axis_index("sub"), lax.axis_index("rng")
    ups = [lax.rem(sub // (1 << level), 2) for level in range(LEVELS)]
    partners = [sub + (1 - 2 * up) * (1 << level) for level, up in enumerate(ups)]
    other = 1 - rng

    def start_row(u, n):
        return pl.multiple_of(jnp.where(rng == 0, u, samples - u - n), HALF)

    def image_copy(c):
        return pltpu.make_async_copy(
            image_ref.at[:, :, pl.ds(pl.multiple_of(start_row(c * CHUNK, CHUNK), CHUNK), CHUNK)],
            image.at[c], image_sem.at[c])

    def out_copy(c):
        return pltpu.make_async_copy(
            image.at[c], out_ref.at[:, :, pl.ds(pl.multiple_of(start_row(c * CHUNK, CHUNK), CHUNK), CHUNK)],
            image_sem.at[c])

    for c in range(chunks):
        image_copy(c).start()

    barrier = pltpu.get_barrier_semaphore()
    neighbours = [(sub, other)] + [(p, rng) for p in partners]
    for device in neighbours:
        pl.semaphore_signal(barrier, inc=1, device_id=device, device_id_type=MESH)

    for level in range(LEVELS):
        for role in range(2):
            child = ups[level] if role == 0 else 1 - ups[level]
            row = 2 * level + role
            share = share_ref[level, pl.ds(child, 1), :]
            whole = lax.rem(37 * (shift_ref[child, 0, level] + 60), 20)
            rows8[0, row : row + 1, :] = share
            rows8[1, row : row + 1, :] = whole.astype(F32) * 0.05 + 1.85 * share
    share = rows8[0]
    turns = rows8[1]
    angle = (2.0 * math.pi) * (turns - jnp.round(turns))
    rows8[2] = jnp.cos(angle) * 0.70710678
    rows8[3] = jnp.sin(angle) * 0.70710678
    sine = jnp.sin(math.pi * share)
    cosine4 = jnp.cos((math.pi / 4) * share)
    sine4 = jnp.sin((math.pi / 4) * share)
    for k in range(-4, 5):
        x = k - share
        window = 0.54 + 0.46 * (math.cos(math.pi * k / 4) * cosine4 + math.sin(math.pi * k / 4) * sine4)
        signed = sine if k % 2 else -sine
        near = x == 0.0
        sinc = jnp.where(near, 1.0, signed / (math.pi * jnp.where(near, 1.0, x)))
        taps[k + 4] = jnp.where(jnp.abs(x) < 4.0, sinc * window, 0.0)

    lane = lax.broadcasted_iota(jnp.int32, (1, BEAMS), 1)
    row128 = lax.broadcasted_iota(jnp.int32, (BEAMS, BEAMS), 0)
    row8 = lax.broadcasted_iota(jnp.int32, (GROUP, BEAMS), 0)

    def weights(level):
        up = ups[level]
        for role in range(2):
            child = up if role == 0 else 1 - up
            row = 2 * level + role
            position = 0.5 * (up * BEAMS + lane).astype(F32)
            position = position + angle_ref[child, 0, level].astype(F32) + fraction_ref[level, pl.ds(child, 1), :]
            cos, sin = rows8[2, row : row + 1, :], rows8[3, row : row + 1, :]
            if role == 0:
                keys = keys_kernel(row128.astype(F32) - position)
                top = jnp.concatenate([keys * cos, keys * sin], axis=1)
                bottom = jnp.concatenate([keys * -sin, keys * cos], axis=1)
            else:
                keys = keys_kernel((row128[:HALF] + HALF * up).astype(F32) - position)
                top = jnp.concatenate(
                    [jnp.concatenate([keys * cos, keys * sin], axis=1),
                     jnp.concatenate([keys * -sin, keys * cos], axis=1)], axis=0)
                beam = HALF - 4 * up + lax.rem(row8, 4)
                keys = keys_kernel(beam.astype(F32) - position)
                real = row8 < 4
                eight = jnp.concatenate(
                    [keys * jnp.where(real, cos, -sin), keys * jnp.where(real, sin, cos)], axis=1)
                bottom = jnp.concatenate([eight] * (BEAMS // GROUP), axis=0)
            for part, block in enumerate((top, bottom)):
                high, low = split(block)
                for place, values in enumerate((high, high, low)):
                    first = 2 * place * BEAMS + part * BEAMS
                    weight[level, role, first : first + BEAMS, :] = values

    outside = start_row(-EDGE, EDGE) + EDGE
    for level in range(LEVELS):
        for role in range(2):
            for plane in range(2):
                steered[level, role, plane, pl.ds(outside, EDGE), :] = jnp.zeros((EDGE, BEAMS), F32)

    def partner_copy(level, c, n):
        rows = PACKED if n == CHUNK else HALF + GROUP
        return pltpu.make_async_remote_copy(
            src_ref=sent.at[level, c, 0:rows, :], dst_ref=got.at[level, c, 0:rows, :], send_sem=send_sem.at[level, c],
            recv_sem=recv_sem.at[level, c], device_id=(partners[level], rng), device_id_type=MESH)

    def halo_copies(level):
        first = start_row(samples - EDGE, EDGE)
        piece = pl.multiple_of(jnp.where(rng == 1, 0, HALF), GROUP) if level % 2 == 0 else 0
        return (
            pltpu.make_async_remote_copy(
                src_ref=cur.at[level, :, pl.ds(first, EDGE), :], dst_ref=own_halo.at[level],
                send_sem=halo_send.at[level, 0], recv_sem=halo_recv.at[level, 0],
                device_id=(sub, other), device_id_type=MESH),
            pltpu.make_async_remote_copy(
                src_ref=sent.at[level, chunks - 1 + level % 2, pl.ds(piece, EDGE + GROUP), :], dst_ref=partner_halo.at[level],
                send_sem=halo_send.at[level, 1], recv_sem=halo_recv.at[level, 1],
                device_id=(partners[level], other), device_id_type=MESH))

    def steer(level, role, x, row):
        high, low = split(x)
        s = jnp.dot(jnp.concatenate([high, low, high], axis=1), weight[level, role], preferred_element_type=F32)
        for plane in range(2):
            steered[level, role, plane, pl.ds(row, x.shape[0]), :] = s[:, plane * BEAMS : (plane + 1) * BEAMS]

    def unpack(main, margins, first_group):
        blocks = []
        for g in range(main.shape[0] // GROUP):
            blocks.append(jnp.where(lane // GROUP == first_group + g, margins, 0.0))
        return jnp.concatenate([main, jnp.concatenate(blocks, axis=0)], axis=1)

    def produce(level, c, u, n, send=True):
        row = start_row(u, n)
        up = ups[level]
        theirs = 1 - up
        near = cur[level, theirs, pl.ds(row, n), :]
        far = pltpu.roll(cur[level, up, pl.ds(row, n), :], HALF, 1)
        main = jnp.where((lane < HALF) == (theirs == 0), near, far)
        first = HALF - 4 * theirs
        real = cur[level, 0, pl.ds(row, n), :]
        imag = cur[level, 1, pl.ds(row, n), :]
        both = jnp.where((lane >= first) & (lane < first + 4), real, pltpu.roll(imag, 4, 1))
        margins = jnp.zeros((GROUP, BEAMS), F32)
        for g in range(n // GROUP):
            turned = pltpu.roll(both[g * GROUP : (g + 1) * GROUP], lax.rem(g * GROUP - first + BEAMS, BEAMS), 1)
            margins = jnp.where(lane // GROUP == g, turned, margins)
        sent[level, c, 0:HALF, :] = main[:HALF]
        sent[level, c, HALF : HALF + GROUP, :] = margins
        if n == CHUNK:
            sent[level, c, HALF + GROUP : PACKED, :] = main[HALF:]
        if send:
            send_out(level, c, n)

    def send_out(level, c, n):
        partner_copy(level, c, n).start()

        def halos():
            for copy in halo_copies(level):
                copy.start()

        if level % 2 == 0:
            if not isinstance(c, int):
                pl.when(c == chunks - 1)(halos)
        elif isinstance(c, int) and c == chunks:
            halos()

    def steer_halo(level):
        for copy in halo_copies(level):
            copy.wait_recv()
        row = start_row(samples, EDGE) + EDGE
        steer(level, 0, jnp.concatenate([own_halo[level, 0], own_halo[level, 1]], axis=1), row)
        if level % 2 == 0:
            main = partner_halo[level, pl.ds(pl.multiple_of(rng * GROUP, GROUP), EDGE), :]
            margins = partner_halo[level, pl.ds(pl.multiple_of((1 - rng) * EDGE, GROUP), GROUP), :]
            steer(level, 1, unpack(main, margins, rng * GROUP), row)
        else:
            steer(level, 1, unpack(partner_halo[level, 0:EDGE, :], partner_halo[level, EDGE:, :], 0), row)

    def shifted(level, role, plane, row, n):
        start = row + (EDGE - 4) + shift_ref[ups[level] if role == 0 else 1 - ups[level], 0, level]
        total = None
        for k in range(9):
            tap = taps[k, 2 * level + role : 2 * level + role + 1, :]
            term = tap * steered[level, role, plane, pl.ds(start + k, n), :]
            total = term if total is None else total + term
        return total

    def merge_own(level, u, n):
        row = start_row(u, n)
        for plane in range(2):
            cur[level + 1, plane, pl.ds(row, n), :] = shifted(level, 0, plane, row, n)

    def merge(level, c, u, n):
        row = start_row(u, n)
        for plane in range(2):
            total = cur[level + 1, plane, pl.ds(row, n), :] + shifted(level, 1, plane, row, n)
            if level + 1 < LEVELS:
                cur[level + 1, plane, pl.ds(row, n), :] = total
            else:
                image[c, plane] = total.T
        if level + 1 < LEVELS:
            produce(level + 1, c, u, n)
        else:
            out_copy(c).start()

    def steer_own(level, u, n):
        row = start_row(u, n)
        own = [cur[level, plane, pl.ds(row, n), :] for plane in range(2)]
        steer(level, 0, jnp.concatenate(own, axis=1), row + EDGE)

    def receive(level, c, u, n):
        partner_copy(level, c, n).wait_recv()
        margins = got[level, c, HALF : HALF + GROUP, :]
        main = got[level, c, 0:HALF, :]
        if n == CHUNK:
            main = jnp.concatenate([main, got[level, c, HALF + GROUP : PACKED, :]], axis=0)
        steer(level, 1, unpack(main, margins, 0), start_row(u, n) + EDGE)

    def consume(level, c):
        if level % 2 == 0:
            steer_own(level, c * CHUNK, CHUNK)

            @pl.when(c == 0)
            def _():
                merge_own(level, 0, HALF)
                receive(level, 0, 0, CHUNK)
                merge(level, 0, 0, HALF)

            @pl.when(c > 0)
            def _():
                merge_own(level, c * CHUNK - HALF, CHUNK)
                receive(level, c, c * CHUNK, CHUNK)
                merge(level, c, c * CHUNK - HALF, CHUNK)

            @pl.when(c == chunks - 1)
            def _():
                steer_halo(level)
                merge_own(level, samples - HALF, HALF)
                merge(level, chunks, samples - HALF, HALF)
        else:
            @pl.when(c == 0)
            def _():
                steer_own(level, 0, HALF)
                receive(level, 0, 0, HALF)

            @pl.when((c > 0) & (c < chunks))
            def _():
                steer_own(level, c * CHUNK - HALF, CHUNK)
                merge_own(level, (c - 1) * CHUNK, CHUNK)
                receive(level, c, c * CHUNK - HALF, CHUNK)

            @pl.when(c == chunks)
            def _():
                steer_own(level, samples - HALF, HALF)
                steer_halo(level)
                merge_own(level, samples - CHUNK, CHUNK)
                receive(level, chunks, samples - HALF, HALF)

            @pl.when(c > 0)
            def _():
                merge(level, c - 1, (c - 1) * CHUNK, CHUNK)

    def take(c, send=True):
        image_copy(c).wait()
        row = start_row(c * CHUNK, CHUNK)
        for plane in range(2):
            cur[0, plane, pl.ds(row, CHUNK), :] = image[c, plane].T
        produce(0, c, c * CHUNK, CHUNK, send)

    for c in range(AHEAD):
        take(c, False)
    weights(0)
    pl.semaphore_wait(barrier, len(neighbours))
    for c in range(AHEAD):
        send_out(0, c, CHUNK)
    for level in range(1, LEVELS):
        weights(level)

    def step(k, carry):
        for level in ORDER:
            if level < 0:
                pl.when(k < chunks)(lambda: take(k))
            else:
                c = k - LAG[level]
                pl.when((c >= 0) & (c < chunks + level % 2))(lambda level=level, c=c: consume(level, c))
        return carry

    lax.fori_loop(AHEAD, chunks + LAG[-1] + 1, step, 0)

    for level in range(LEVELS):
        first = level % 2

        def finish(c, carry):
            partner_copy(level, c, CHUNK).wait_send()
            return carry

        lax.fori_loop(first, chunks, finish, 0)
        if first:
            partner_copy(level, 0, HALF).wait_send()
            partner_copy(level, chunks, HALF).wait_send()
        for copy in halo_copies(level):
            copy.wait_send()
    for c in range(chunks):
        out_copy(c).wait()


def per_device(image, angle_offset, angle_fraction, integer_distance_shifts, subcell_distance_shares):
    samples = image.shape[2]
    chunks = samples // CHUNK
    vmem, smem = pl.BlockSpec(memory_space=pltpu.VMEM), pl.BlockSpec(memory_space=pltpu.SMEM)
    return pl.pallas_call(
        lambda *refs: kernel(samples, *refs),
        out_shape=jax.ShapeDtypeStruct(image.shape, F32),
        in_specs=[smem, smem, pl.BlockSpec(memory_space=pltpu.HBM), vmem, vmem],
        out_specs=pl.BlockSpec(memory_space=pltpu.HBM),
        scratch_shapes=[
            pltpu.VMEM((chunks, 2, BEAMS, CHUNK), F32),
            pltpu.VMEM((LEVELS + 1, 2, samples, BEAMS), F32),
            pltpu.VMEM((LEVELS, chunks + 1, PACKED, BEAMS), F32),
            pltpu.VMEM((LEVELS, chunks + 1, PACKED, BEAMS), F32),
            pltpu.VMEM((LEVELS, 2, EDGE, BEAMS), F32),
            pltpu.VMEM((LEVELS, EDGE + GROUP, BEAMS), F32),
            pltpu.VMEM((LEVELS, 2, 2, samples + 2 * EDGE, BEAMS), F32),
            pltpu.VMEM((LEVELS, 2, 6 * BEAMS, 2 * BEAMS), BF16),
            pltpu.VMEM((4, 2 * LEVELS, BEAMS), F32),
            pltpu.VMEM((9, 2 * LEVELS, BEAMS), F32),
            pltpu.SemaphoreType.DMA((chunks,)),
            pltpu.SemaphoreType.DMA((LEVELS, chunks + 1)),
            pltpu.SemaphoreType.DMA((LEVELS, chunks + 1)),
            pltpu.SemaphoreType.DMA((LEVELS, 2)),
            pltpu.SemaphoreType.DMA((LEVELS, 2)),
        ],
        compiler_params=pltpu.CompilerParams(
            collective_id=0, has_side_effects=True, vmem_limit_bytes=56 * 1024 * 1024),
    )(jnp.transpose(angle_offset, (1, 2, 0)), jnp.transpose(integer_distance_shifts, (1, 2, 0)), image, angle_fraction, subcell_distance_shares)


def solution(mesh):
    placed = (P(None, "sub", "rng"),) + (P(None, None, "sub"),) * 4
    return jax.shard_map(
        per_device, mesh=mesh, in_specs=placed, out_specs=P(None, "sub", "rng"), check_vma=False)
```

```python
import math

import jax
import jax.numpy as jnp
from jax import lax
from jax.experimental import pallas as pl
from jax.experimental.pallas import tpu as pltpu
from jax.sharding import PartitionSpec as P

LEVELS = 4
BEAMS = 128
HALF = 64
EDGE = 64
CHUNK = 128
GROUP = 8
PACKED = CHUNK + GROUP
AHEAD = 2
LAG = (2, 3, 6, 10)
WEIGHTS = {1: (3, 2), 2: (5, 3)}
ORDER = (0, -1, 1, 2, 3)
MESH = pl.DeviceIdType.MESH
F32, BF16 = jnp.float32, jnp.bfloat16


def keys_kernel(distance):
    m = jnp.abs(distance)
    inner = (1.5 * m - 2.5) * m * m + 1.0
    outer = ((-0.5 * m + 2.5) * m - 4.0) * m + 2.0
    return jnp.where(m < 1.0, inner, jnp.where(m < 2.0, outer, 0.0))


def split(x):
    high = x.astype(BF16)
    return high, (x - high.astype(F32)).astype(BF16)


def kernel(samples, angle_ref, shift_ref, image_ref, fraction_ref, share_ref, out_ref, image, cur, sent, got, own_halo,
           partner_halo, steered, weight, rows8, taps, image_sem, send_sem, recv_sem, halo_send, halo_recv):
    chunks = samples // CHUNK
    sub, rng = lax.axis_index("sub"), lax.axis_index("rng")
    ups = [lax.rem(sub // (1 << level), 2) for level in range(LEVELS)]
    partners = [sub + (1 - 2 * up) * (1 << level) for level, up in enumerate(ups)]
    other = 1 - rng

    def start_row(u, n):
        return pl.multiple_of(jnp.where(rng == 0, u, samples - u - n), HALF)

    def image_copy(c):
        return pltpu.make_async_copy(
            image_ref.at[:, :, pl.ds(pl.multiple_of(start_row(c * CHUNK, CHUNK), CHUNK), CHUNK)],
            image.at[c], image_sem.at[c])

    def out_copy(c):
        return pltpu.make_async_copy(
            image.at[c], out_ref.at[:, :, pl.ds(pl.multiple_of(start_row(c * CHUNK, CHUNK), CHUNK), CHUNK)],
            image_sem.at[c])

    for c in range(chunks):
        image_copy(c).start()

    barrier = pltpu.get_barrier_semaphore()
    neighbours = [(sub, other)] + [(p, rng) for p in partners]
    for device in neighbours:
        pl.semaphore_signal(barrier, inc=1, device_id=device, device_id_type=MESH)

    for level in range(LEVELS):
        for role in range(2):
            child = ups[level] if role == 0 else 1 - ups[level]
            row = 2 * level + role
            share = share_ref[level, pl.ds(child, 1), :]
            whole = lax.rem(37 * (shift_ref[child, 0, level] + 60), 20)
            rows8[0, row : row + 1, :] = share
            rows8[1, row : row + 1, :] = whole.astype(F32) * 0.05 + 1.85 * share
    share = rows8[0]
    turns = rows8[1]
    angle = (2.0 * math.pi) * (turns - jnp.round(turns))
    rows8[2] = jnp.cos(angle) * 0.70710678
    rows8[3] = jnp.sin(angle) * 0.70710678
    sine = jnp.sin(math.pi * share)
    cosine4 = jnp.cos((math.pi / 4) * share)
    sine4 = jnp.sin((math.pi / 4) * share)
    for k in range(-4, 5):
        x = k - share
        window = 0.54 + 0.46 * (math.cos(math.pi * k / 4) * cosine4 + math.sin(math.pi * k / 4) * sine4)
        signed = sine if k % 2 else -sine
        near = x == 0.0
        sinc = jnp.where(near, 1.0, signed / (math.pi * jnp.where(near, 1.0, x)))
        taps[k + 4] = jnp.where(jnp.abs(x) < 4.0, sinc * window, 0.0)

    lane = lax.broadcasted_iota(jnp.int32, (1, BEAMS), 1)
    row128 = lax.broadcasted_iota(jnp.int32, (BEAMS, BEAMS), 0)
    row8 = lax.broadcasted_iota(jnp.int32, (GROUP, BEAMS), 0)

    def weights(level):
        up = ups[level]
        for role in range(2):
            child = up if role == 0 else 1 - up
            row = 2 * level + role
            position = 0.5 * (up * BEAMS + lane).astype(F32)
            position = position + angle_ref[child, 0, level].astype(F32) + fraction_ref[level, pl.ds(child, 1), :]
            cos, sin = rows8[2, row : row + 1, :], rows8[3, row : row + 1, :]
            if role == 0:
                keys = keys_kernel(row128.astype(F32) - position)
                top = jnp.concatenate([keys * cos, keys * sin], axis=1)
                bottom = jnp.concatenate([keys * -sin, keys * cos], axis=1)
            else:
                keys = keys_kernel((row128[:HALF] + HALF * up).astype(F32) - position)
                top = jnp.concatenate(
                    [jnp.concatenate([keys * cos, keys * sin], axis=1),
                     jnp.concatenate([keys * -sin, keys * cos], axis=1)], axis=0)
                beam = HALF - 4 * up + lax.rem(row8, 4)
                keys = keys_kernel(beam.astype(F32) - position)
                real = row8 < 4
                eight = jnp.concatenate(
                    [keys * jnp.where(real, cos, -sin), keys * jnp.where(real, sin, cos)], axis=1)
                bottom = jnp.concatenate([eight] * (BEAMS // GROUP), axis=0)
            for part, block in enumerate((top, bottom)):
                high, low = split(block)
                for place, values in enumerate((high, high, low)):
                    first = 2 * place * BEAMS + part * BEAMS
                    weight[level, role, first : first + BEAMS, :] = values

    outside = start_row(-EDGE, EDGE) + EDGE
    for level in range(LEVELS):
        for role in range(2):
            for plane in range(2):
                steered[level, role, plane, pl.ds(outside, EDGE), :] = jnp.zeros((EDGE, BEAMS), F32)

    def partner_copy(level, c, n):
        rows = PACKED if n == CHUNK else HALF + GROUP
        return pltpu.make_async_remote_copy(
            src_ref=sent.at[level, c, 0:rows, :], dst_ref=got.at[level, c, 0:rows, :], send_sem=send_sem.at[level, c],
            recv_sem=recv_sem.at[level, c], device_id=(partners[level], rng), device_id_type=MESH)

    def halo_copies(level):
        first = start_row(samples - EDGE, EDGE)
        piece = pl.multiple_of(jnp.where(rng == 1, 0, HALF), GROUP) if level % 2 == 0 else 0
        return (
            pltpu.make_async_remote_copy(
                src_ref=cur.at[level, :, pl.ds(first, EDGE), :], dst_ref=own_halo.at[level],
                send_sem=halo_send.at[level, 0], recv_sem=halo_recv.at[level, 0],
                device_id=(sub, other), device_id_type=MESH),
            pltpu.make_async_remote_copy(
                src_ref=sent.at[level, chunks - 1 + level % 2, pl.ds(piece, EDGE + GROUP), :], dst_ref=partner_halo.at[level],
                send_sem=halo_send.at[level, 1], recv_sem=halo_recv.at[level, 1],
                device_id=(partners[level], other), device_id_type=MESH))

    def steer(level, role, x, row):
        high, low = split(x)
        s = jnp.dot(jnp.concatenate([high, low, high], axis=1), weight[level, role], preferred_element_type=F32)
        for plane in range(2):
            steered[level, role, plane, pl.ds(row, x.shape[0]), :] = s[:, plane * BEAMS : (plane + 1) * BEAMS]

    def unpack(main, margins, first_group):
        blocks = []
        for g in range(main.shape[0] // GROUP):
            blocks.append(jnp.where(lane // GROUP == first_group + g, margins, 0.0))
        return jnp.concatenate([main, jnp.concatenate(blocks, axis=0)], axis=1)

    def produce(level, c, u, n, send=True):
        row = start_row(u, n)
        up = ups[level]
        theirs = 1 - up
        near = cur[level, theirs, pl.ds(row, n), :]
        far = pltpu.roll(cur[level, up, pl.ds(row, n), :], HALF, 1)
        main = jnp.where((lane < HALF) == (theirs == 0), near, far)
        first = HALF - 4 * theirs
        real = cur[level, 0, pl.ds(row, n), :]
        imag = cur[level, 1, pl.ds(row, n), :]
        both = jnp.where((lane >= first) & (lane < first + 4), real, pltpu.roll(imag, 4, 1))
        margins = jnp.zeros((GROUP, BEAMS), F32)
        for g in range(n // GROUP):
            turned = pltpu.roll(both[g * GROUP : (g + 1) * GROUP], lax.rem(g * GROUP - first + BEAMS, BEAMS), 1)
            margins = jnp.where(lane // GROUP == g, turned, margins)
        sent[level, c, 0:HALF, :] = main[:HALF]
        sent[level, c, HALF : HALF + GROUP, :] = margins
        if n == CHUNK:
            sent[level, c, HALF + GROUP : PACKED, :] = main[HALF:]
        if send:
            send_out(level, c, n)

    def send_out(level, c, n):
        partner_copy(level, c, n).start()

        def halos():
            for copy in halo_copies(level):
                copy.start()

        if level % 2 == 0:
            if not isinstance(c, int):
                pl.when(c == chunks - 1)(halos)
        elif isinstance(c, int) and c == chunks:
            halos()

    def steer_halo(level):
        for copy in halo_copies(level):
            copy.wait_recv()
        row = start_row(samples, EDGE) + EDGE
        steer(level, 0, jnp.concatenate([own_halo[level, 0], own_halo[level, 1]], axis=1), row)
        if level % 2 == 0:
            main = partner_halo[level, pl.ds(pl.multiple_of(rng * GROUP, GROUP), EDGE), :]
            margins = partner_halo[level, pl.ds(pl.multiple_of((1 - rng) * EDGE, GROUP), GROUP), :]
            steer(level, 1, unpack(main, margins, rng * GROUP), row)
        else:
            steer(level, 1, unpack(partner_halo[level, 0:EDGE, :], partner_halo[level, EDGE:, :], 0), row)

    def shifted(level, role, plane, row, n):
        start = row + (EDGE - 4) + shift_ref[ups[level] if role == 0 else 1 - ups[level], 0, level]
        total = None
        for k in range(9):
            tap = taps[k, 2 * level + role : 2 * level + role + 1, :]
            term = tap * steered[level, role, plane, pl.ds(start + k, n), :]
            total = term if total is None else total + term
        return total

    def merge_own(level, u, n):
        row = start_row(u, n)
        for plane in range(2):
            cur[level + 1, plane, pl.ds(row, n), :] = shifted(level, 0, plane, row, n)

    def merge(level, c, u, n):
        row = start_row(u, n)
        for plane in range(2):
            total = cur[level + 1, plane, pl.ds(row, n), :] + shifted(level, 1, plane, row, n)
            if level + 1 < LEVELS:
                cur[level + 1, plane, pl.ds(row, n), :] = total
            else:
                image[c, plane] = total.T
        if level + 1 < LEVELS:
            produce(level + 1, c, u, n)
        else:
            out_copy(c).start()

    def steer_own(level, u, n):
        row = start_row(u, n)
        own = [cur[level, plane, pl.ds(row, n), :] for plane in range(2)]
        steer(level, 0, jnp.concatenate(own, axis=1), row + EDGE)

    def receive(level, c, u, n):
        partner_copy(level, c, n).wait_recv()
        margins = got[level, c, HALF : HALF + GROUP, :]
        main = got[level, c, 0:HALF, :]
        if n == CHUNK:
            main = jnp.concatenate([main, got[level, c, HALF + GROUP : PACKED, :]], axis=0)
        steer(level, 1, unpack(main, margins, 0), start_row(u, n) + EDGE)

    def consume(level, c):
        if level % 2 == 0:
            steer_own(level, c * CHUNK, CHUNK)

            @pl.when(c == 0)
            def _():
                merge_own(level, 0, HALF)
                receive(level, 0, 0, CHUNK)
                merge(level, 0, 0, HALF)

            @pl.when(c > 0)
            def _():
                merge_own(level, c * CHUNK - HALF, CHUNK)
                receive(level, c, c * CHUNK, CHUNK)
                merge(level, c, c * CHUNK - HALF, CHUNK)

            @pl.when(c == chunks - 1)
            def _():
                steer_halo(level)
                merge_own(level, samples - HALF, HALF)
                merge(level, chunks, samples - HALF, HALF)
        else:
            @pl.when(c == 0)
            def _():
                steer_own(level, 0, HALF)
                receive(level, 0, 0, HALF)

            @pl.when((c > 0) & (c < chunks))
            def _():
                steer_own(level, c * CHUNK - HALF, CHUNK)
                merge_own(level, (c - 1) * CHUNK, CHUNK)
                receive(level, c, c * CHUNK - HALF, CHUNK)

            @pl.when(c == chunks)
            def _():
                steer_own(level, samples - HALF, HALF)
                steer_halo(level)
                merge_own(level, samples - CHUNK, CHUNK)
                receive(level, chunks, samples - HALF, HALF)

            @pl.when(c > 0)
            def _():
                merge(level, c - 1, (c - 1) * CHUNK, CHUNK)

    def take(c, send=True):
        image_copy(c).wait()
        row = start_row(c * CHUNK, CHUNK)
        for plane in range(2):
            cur[0, plane, pl.ds(row, CHUNK), :] = image[c, plane].T
        produce(0, c, c * CHUNK, CHUNK, send)

    for c in range(AHEAD):
        take(c, False)
    weights(0)
    pl.semaphore_wait(barrier, len(neighbours))
    for c in range(AHEAD):
        send_out(0, c, CHUNK)
    weights(1)

    def step(k, carry):
        for level in ORDER:
            if level in WEIGHTS:
                pl.when(k == WEIGHTS[level][0])(lambda level=level: weights(WEIGHTS[level][1]))
            if level < 0:
                pl.when(k < chunks)(lambda: take(k))
            else:
                c = k - LAG[level]
                pl.when((c >= 0) & (c < chunks + level % 2))(lambda level=level, c=c: consume(level, c))
        return carry

    lax.fori_loop(AHEAD, chunks + LAG[-1] + 1, step, 0)

    for level in range(LEVELS):
        first = level % 2

        def finish(c, carry):
            partner_copy(level, c, CHUNK).wait_send()
            return carry

        lax.fori_loop(first, chunks, finish, 0)
        if first:
            partner_copy(level, 0, HALF).wait_send()
            partner_copy(level, chunks, HALF).wait_send()
        for copy in halo_copies(level):
            copy.wait_send()
    for c in range(chunks):
        out_copy(c).wait()


def per_device(image, angle_offset, angle_fraction, integer_distance_shifts, subcell_distance_shares):
    samples = image.shape[2]
    chunks = samples // CHUNK
    vmem, smem = pl.BlockSpec(memory_space=pltpu.VMEM), pl.BlockSpec(memory_space=pltpu.SMEM)
    return pl.pallas_call(
        lambda *refs: kernel(samples, *refs),
        out_shape=jax.ShapeDtypeStruct(image.shape, F32),
        in_specs=[smem, smem, pl.BlockSpec(memory_space=pltpu.HBM), vmem, vmem],
        out_specs=pl.BlockSpec(memory_space=pltpu.HBM),
        scratch_shapes=[
            pltpu.VMEM((chunks, 2, BEAMS, CHUNK), F32),
            pltpu.VMEM((LEVELS + 1, 2, samples, BEAMS), F32),
            pltpu.VMEM((LEVELS, chunks + 1, PACKED, BEAMS), F32),
            pltpu.VMEM((LEVELS, chunks + 1, PACKED, BEAMS), F32),
            pltpu.VMEM((LEVELS, 2, EDGE, BEAMS), F32),
            pltpu.VMEM((LEVELS, EDGE + GROUP, BEAMS), F32),
            pltpu.VMEM((LEVELS, 2, 2, samples + 2 * EDGE, BEAMS), F32),
            pltpu.VMEM((LEVELS, 2, 6 * BEAMS, 2 * BEAMS), BF16),
            pltpu.VMEM((4, 2 * LEVELS, BEAMS), F32),
            pltpu.VMEM((9, 2 * LEVELS, BEAMS), F32),
            pltpu.SemaphoreType.DMA((chunks,)),
            pltpu.SemaphoreType.DMA((LEVELS, chunks + 1)),
            pltpu.SemaphoreType.DMA((LEVELS, chunks + 1)),
            pltpu.SemaphoreType.DMA((LEVELS, 2)),
            pltpu.SemaphoreType.DMA((LEVELS, 2)),
        ],
        compiler_params=pltpu.CompilerParams(
            collective_id=0, has_side_effects=True, vmem_limit_bytes=56 * 1024 * 1024),
    )(jnp.transpose(angle_offset, (1, 2, 0)), jnp.transpose(integer_distance_shifts, (1, 2, 0)), image, angle_fraction, subcell_distance_shares)


def solution(mesh):
    placed = (P(None, "sub", "rng"),) + (P(None, None, "sub"),) * 4
    return jax.shard_map(
        per_device, mesh=mesh, in_specs=placed, out_specs=P(None, "sub", "rng"), check_vma=False)
```

```python
import math

import jax
import jax.numpy as jnp
from jax import lax
from jax.experimental import pallas as pl
from jax.experimental.pallas import tpu as pltpu
from jax.sharding import PartitionSpec as P

LEVELS = 4
BEAMS = 128
HALF = 64
EDGE = 64
CHUNK = 128
GROUP = 8
PACKED = CHUNK + GROUP
AHEAD = 2
LAG = (2, 3, 6, 10)
WEIGHTS = {1: (3, 2), 2: (5, 3)}
ORDER = (0, -1, 1, 2, 3)
MESH = pl.DeviceIdType.MESH
F32, BF16 = jnp.float32, jnp.bfloat16


def keys_kernel(distance):
    m = jnp.abs(distance)
    inner = (1.5 * m - 2.5) * m * m + 1.0
    outer = ((-0.5 * m + 2.5) * m - 4.0) * m + 2.0
    return jnp.where(m < 1.0, inner, jnp.where(m < 2.0, outer, 0.0))


def split(x):
    high = x.astype(BF16)
    return high, (x - high.astype(F32)).astype(BF16)


def kernel(samples, angle_ref, shift_ref, image_ref, fraction_ref, share_ref, out_ref, image, cur, sent, got, own_halo,
           partner_halo, steered, weight, rows8, taps, image_sem, send_sem, recv_sem, halo_send, halo_recv):
    chunks = samples // CHUNK
    sub, rng = lax.axis_index("sub"), lax.axis_index("rng")
    ups = [lax.rem(sub // (1 << level), 2) for level in range(LEVELS)]
    partners = [sub + (1 - 2 * up) * (1 << level) for level, up in enumerate(ups)]
    other = 1 - rng

    def start_row(u, n):
        return pl.multiple_of(jnp.where(rng == 0, u, samples - u - n), HALF)

    def image_copy(c):
        return pltpu.make_async_copy(
            image_ref.at[:, :, pl.ds(pl.multiple_of(start_row(c * CHUNK, CHUNK), CHUNK), CHUNK)],
            image.at[c], image_sem.at[c])

    def out_copy(c):
        return pltpu.make_async_copy(
            image.at[c], out_ref.at[:, :, pl.ds(pl.multiple_of(start_row(c * CHUNK, CHUNK), CHUNK), CHUNK)],
            image_sem.at[c])

    for c in range(chunks):
        image_copy(c).start()

    barrier = pltpu.get_barrier_semaphore()
    neighbours = [(sub, other)] + [(p, rng) for p in partners]
    for device in neighbours:
        pl.semaphore_signal(barrier, inc=1, device_id=device, device_id_type=MESH)

    for level in range(LEVELS):
        for role in range(2):
            child = ups[level] if role == 0 else 1 - ups[level]
            row = 2 * level + role
            share = share_ref[level, pl.ds(child, 1), :]
            whole = lax.rem(37 * (shift_ref[child, 0, level] + 60), 20)
            rows8[0, row : row + 1, :] = share
            rows8[1, row : row + 1, :] = whole.astype(F32) * 0.05 + 1.85 * share
    share = rows8[0]
    turns = rows8[1]
    angle = (2.0 * math.pi) * (turns - jnp.round(turns))
    rows8[2] = jnp.cos(angle) * 0.70710678
    rows8[3] = jnp.sin(angle) * 0.70710678
    sine = jnp.sin(math.pi * share)
    cosine4 = jnp.cos((math.pi / 4) * share)
    sine4 = jnp.sin((math.pi / 4) * share)
    for k in range(-4, 5):
        x = k - share
        window = 0.54 + 0.46 * (math.cos(math.pi * k / 4) * cosine4 + math.sin(math.pi * k / 4) * sine4)
        signed = sine if k % 2 else -sine
        near = x == 0.0
        sinc = jnp.where(near, 1.0, signed / (math.pi * jnp.where(near, 1.0, x)))
        taps[k + 4] = jnp.where(jnp.abs(x) < 4.0, sinc * window, 0.0)

    lane = lax.broadcasted_iota(jnp.int32, (1, BEAMS), 1)
    row128 = lax.broadcasted_iota(jnp.int32, (BEAMS, BEAMS), 0)
    row8 = lax.broadcasted_iota(jnp.int32, (GROUP, BEAMS), 0)

    def weights(level):
        up = ups[level]
        for role in range(2):
            child = up if role == 0 else 1 - up
            row = 2 * level + role
            position = 0.5 * (up * BEAMS + lane).astype(F32)
            position = position + angle_ref[child, 0, level].astype(F32) + fraction_ref[level, pl.ds(child, 1), :]
            cos, sin = rows8[2, row : row + 1, :], rows8[3, row : row + 1, :]
            if role == 0:
                keys = keys_kernel(row128.astype(F32) - position)
                top = jnp.concatenate([keys * cos, keys * sin], axis=1)
                bottom = jnp.concatenate([keys * -sin, keys * cos], axis=1)
            else:
                keys = keys_kernel((row128[:HALF] + HALF * up).astype(F32) - position)
                top = jnp.concatenate(
                    [jnp.concatenate([keys * cos, keys * sin], axis=1),
                     jnp.concatenate([keys * -sin, keys * cos], axis=1)], axis=0)
                beam = HALF - 4 * up + lax.rem(row8, 4)
                keys = keys_kernel(beam.astype(F32) - position)
                real = row8 < 4
                eight = jnp.concatenate(
                    [keys * jnp.where(real, cos, -sin), keys * jnp.where(real, sin, cos)], axis=1)
                bottom = jnp.concatenate([eight] * (BEAMS // GROUP), axis=0)
            for part, block in enumerate((top, bottom)):
                high, low = split(block)
                for place, values in enumerate((high, high, low)):
                    first = 2 * place * BEAMS + part * BEAMS
                    weight[level, role, first : first + BEAMS, :] = values

    outside = start_row(-EDGE, EDGE) + EDGE
    for level in range(LEVELS):
        for role in range(2):
            for plane in range(2):
                steered[level, role, plane, pl.ds(outside, EDGE), :] = jnp.zeros((EDGE, BEAMS), F32)

    def partner_copy(level, c, n):
        rows = PACKED if n == CHUNK else HALF + GROUP
        return pltpu.make_async_remote_copy(
            src_ref=sent.at[level, c, 0:rows, :], dst_ref=got.at[level, c, 0:rows, :], send_sem=send_sem.at[level, c],
            recv_sem=recv_sem.at[level, c], device_id=(partners[level], rng), device_id_type=MESH)

    def halo_copies(level):
        first = start_row(samples - EDGE, EDGE)
        piece = pl.multiple_of(jnp.where(rng == 1, 0, HALF), GROUP) if level % 2 == 0 else 0
        if level == LEVELS - 1:
            source, target = got.at[level, chunks, 0 : EDGE + GROUP, :], sub
        else:
            source, target = sent.at[level, chunks - 1 + level % 2, pl.ds(piece, EDGE + GROUP), :], partners[level]
        return (
            pltpu.make_async_remote_copy(
                src_ref=cur.at[level, :, pl.ds(first, EDGE), :], dst_ref=own_halo.at[level],
                send_sem=halo_send.at[level, 0], recv_sem=halo_recv.at[level, 0],
                device_id=(sub, other), device_id_type=MESH),
            pltpu.make_async_remote_copy(
                src_ref=source, dst_ref=partner_halo.at[level],
                send_sem=halo_send.at[level, 1], recv_sem=halo_recv.at[level, 1],
                device_id=(target, other), device_id_type=MESH))

    def steer(level, role, x, row):
        high, low = split(x)
        s = jnp.dot(jnp.concatenate([high, low, high], axis=1), weight[level, role], preferred_element_type=F32)
        for plane in range(2):
            steered[level, role, plane, pl.ds(row, x.shape[0]), :] = s[:, plane * BEAMS : (plane + 1) * BEAMS]

    def unpack(main, margins, first_group):
        blocks = []
        for g in range(main.shape[0] // GROUP):
            blocks.append(jnp.where(lane // GROUP == first_group + g, margins, 0.0))
        return jnp.concatenate([main, jnp.concatenate(blocks, axis=0)], axis=1)

    def produce(level, c, u, n, send=True):
        row = start_row(u, n)
        up = ups[level]
        theirs = 1 - up
        near = cur[level, theirs, pl.ds(row, n), :]
        far = pltpu.roll(cur[level, up, pl.ds(row, n), :], HALF, 1)
        main = jnp.where((lane < HALF) == (theirs == 0), near, far)
        first = HALF - 4 * theirs
        real = cur[level, 0, pl.ds(row, n), :]
        imag = cur[level, 1, pl.ds(row, n), :]
        both = jnp.where((lane >= first) & (lane < first + 4), real, pltpu.roll(imag, 4, 1))
        margins = jnp.zeros((GROUP, BEAMS), F32)
        for g in range(n // GROUP):
            turned = pltpu.roll(both[g * GROUP : (g + 1) * GROUP], lax.rem(g * GROUP - first + BEAMS, BEAMS), 1)
            margins = jnp.where(lane // GROUP == g, turned, margins)
        sent[level, c, 0:HALF, :] = main[:HALF]
        sent[level, c, HALF : HALF + GROUP, :] = margins
        if n == CHUNK:
            sent[level, c, HALF + GROUP : PACKED, :] = main[HALF:]
        if send:
            send_out(level, c, n)

    def send_out(level, c, n):
        partner_copy(level, c, n).start()

        def halos():
            for copy in halo_copies(level)[: 1 if level == LEVELS - 1 else 2]:
                copy.start()

        if level % 2 == 0:
            if not isinstance(c, int):
                pl.when(c == chunks - 1)(halos)
        elif isinstance(c, int) and c == chunks:
            halos()

    def steer_halo(level):
        for copy in halo_copies(level):
            copy.wait_recv()
        row = start_row(samples, EDGE) + EDGE
        steer(level, 0, jnp.concatenate([own_halo[level, 0], own_halo[level, 1]], axis=1), row)
        if level % 2 == 0:
            main = partner_halo[level, pl.ds(pl.multiple_of(rng * GROUP, GROUP), EDGE), :]
            margins = partner_halo[level, pl.ds(pl.multiple_of((1 - rng) * EDGE, GROUP), GROUP), :]
            steer(level, 1, unpack(main, margins, rng * GROUP), row)
        else:
            steer(level, 1, unpack(partner_halo[level, 0:EDGE, :], partner_halo[level, EDGE:, :], 0), row)

    def shifted(level, role, plane, row, n):
        start = row + (EDGE - 4) + shift_ref[ups[level] if role == 0 else 1 - ups[level], 0, level]
        total = None
        for k in range(9):
            tap = taps[k, 2 * level + role : 2 * level + role + 1, :]
            term = tap * steered[level, role, plane, pl.ds(start + k, n), :]
            total = term if total is None else total + term
        return total

    def merge_own(level, u, n):
        row = start_row(u, n)
        for plane in range(2):
            cur[level + 1, plane, pl.ds(row, n), :] = shifted(level, 0, plane, row, n)

    def merge(level, c, u, n):
        row = start_row(u, n)
        for plane in range(2):
            total = cur[level + 1, plane, pl.ds(row, n), :] + shifted(level, 1, plane, row, n)
            if level + 1 < LEVELS:
                cur[level + 1, plane, pl.ds(row, n), :] = total
            else:
                image[c, plane] = total.T
        if level + 1 < LEVELS:
            produce(level + 1, c, u, n)
        else:
            out_copy(c).start()

    def steer_own(level, u, n):
        row = start_row(u, n)
        own = [cur[level, plane, pl.ds(row, n), :] for plane in range(2)]
        steer(level, 0, jnp.concatenate(own, axis=1), row + EDGE)

    def receive(level, c, u, n, here=False):
        if not here:
            partner_copy(level, c, n).wait_recv()
        margins = got[level, c, HALF : HALF + GROUP, :]
        main = got[level, c, 0:HALF, :]
        if n == CHUNK:
            main = jnp.concatenate([main, got[level, c, HALF + GROUP : PACKED, :]], axis=0)
        steer(level, 1, unpack(main, margins, 0), start_row(u, n) + EDGE)

    def consume_last(level, before_wait=lambda: None):
        steer_own(level, samples - HALF, HALF)
        steer_halo(level)
        merge_own(level, samples - CHUNK, CHUNK)
        before_wait()
        receive(level, chunks, samples - HALF, HALF, here=level == LEVELS - 1)

    def hand_on():
        partner_copy(LEVELS - 1, chunks, HALF).wait_recv()
        halo_copies(LEVELS - 1)[1].start()

    def consume(level, c):
        if level % 2 == 0:
            steer_own(level, c * CHUNK, CHUNK)

            @pl.when(c == 0)
            def _():
                merge_own(level, 0, HALF)
                receive(level, 0, 0, CHUNK)
                merge(level, 0, 0, HALF)

            @pl.when((c > 0) & (c < chunks - 1))
            def _():
                merge_own(level, c * CHUNK - HALF, CHUNK)
                receive(level, c, c * CHUNK, CHUNK)
                merge(level, c, c * CHUNK - HALF, CHUNK)

            @pl.when(c == chunks - 1)
            def _():
                merge_own(level, c * CHUNK - HALF, CHUNK)
                receive(level, c, c * CHUNK, CHUNK)
                if level == 0:
                    merge(level, c, c * CHUNK - HALF, CHUNK)
                steer_halo(level)
                merge_own(level, samples - HALF, HALF)
                merge(level, chunks, samples - HALF, HALF)
                if level != 0:
                    merge(level, c, c * CHUNK - HALF, CHUNK)
        else:
            @pl.when(c == 0)
            def _():
                steer_own(level, 0, HALF)
                receive(level, 0, 0, HALF)

            @pl.when((c > 0) & (c < chunks))
            def _():
                steer_own(level, c * CHUNK - HALF, CHUNK)
                merge_own(level, (c - 1) * CHUNK, CHUNK)
                if level == LEVELS - 1:
                    pl.when(c == chunks - 1)(hand_on)
                receive(level, c, c * CHUNK - HALF, CHUNK)

            if level < LEVELS - 1:
                pl.when(c == chunks)(lambda: consume_last(level))

            @pl.when(c > 0)
            def _():
                merge(level, c - 1, (c - 1) * CHUNK, CHUNK)

    def take(c, send=True):
        image_copy(c).wait()
        row = start_row(c * CHUNK, CHUNK)
        for plane in range(2):
            cur[0, plane, pl.ds(row, CHUNK), :] = image[c, plane].T
        produce(0, c, c * CHUNK, CHUNK, send)

    for c in range(AHEAD):
        take(c, False)
    weights(0)
    pl.semaphore_wait(barrier, len(neighbours))
    for c in range(AHEAD):
        send_out(0, c, CHUNK)
    weights(1)

    def step(k, carry):
        for level in ORDER:
            if level in WEIGHTS:
                pl.when(k == WEIGHTS[level][0])(lambda level=level: weights(WEIGHTS[level][1]))
            if level < 0:
                pl.when(k < chunks)(lambda: take(k))
            else:
                c = k - LAG[level]
                last = chunks + (level == 1)
                pl.when((c >= 0) & (c < last))(lambda level=level, c=c: consume(level, c))
        return carry

    lax.fori_loop(AHEAD, chunks + LAG[-1], step, 0)

    def sent_all(levels):
        for level in levels:
            first = level % 2

            def finish(c, carry):
                partner_copy(level, c, CHUNK).wait_send()
                return carry

            lax.fori_loop(first, chunks, finish, 0)
            if first:
                partner_copy(level, 0, HALF).wait_send()
                partner_copy(level, chunks, HALF).wait_send()
            for copy in halo_copies(level):
                copy.wait_send()

    def before_wait():
        sent_all(range(LEVELS - 1))
        for c in range(chunks - 1):
            out_copy(c).wait()

    consume_last(LEVELS - 1, before_wait)
    merge(LEVELS - 1, chunks - 1, samples - CHUNK, CHUNK)
    sent_all((LEVELS - 1,))
    out_copy(chunks - 1).wait()


def per_device(image, angle_offset, angle_fraction, integer_distance_shifts, subcell_distance_shares):
    samples = image.shape[2]
    chunks = samples // CHUNK
    vmem, smem = pl.BlockSpec(memory_space=pltpu.VMEM), pl.BlockSpec(memory_space=pltpu.SMEM)
    return pl.pallas_call(
        lambda *refs: kernel(samples, *refs),
        out_shape=jax.ShapeDtypeStruct(image.shape, F32),
        in_specs=[smem, smem, pl.BlockSpec(memory_space=pltpu.HBM), vmem, vmem],
        out_specs=pl.BlockSpec(memory_space=pltpu.HBM),
        scratch_shapes=[
            pltpu.VMEM((chunks, 2, BEAMS, CHUNK), F32),
            pltpu.VMEM((LEVELS + 1, 2, samples, BEAMS), F32),
            pltpu.VMEM((LEVELS, chunks + 1, PACKED, BEAMS), F32),
            pltpu.VMEM((LEVELS, chunks + 1, PACKED, BEAMS), F32),
            pltpu.VMEM((LEVELS, 2, EDGE, BEAMS), F32),
            pltpu.VMEM((LEVELS, EDGE + GROUP, BEAMS), F32),
            pltpu.VMEM((LEVELS, 2, 2, samples + 2 * EDGE, BEAMS), F32),
            pltpu.VMEM((LEVELS, 2, 6 * BEAMS, 2 * BEAMS), BF16),
            pltpu.VMEM((4, 2 * LEVELS, BEAMS), F32),
            pltpu.VMEM((9, 2 * LEVELS, BEAMS), F32),
            pltpu.SemaphoreType.DMA((chunks,)),
            pltpu.SemaphoreType.DMA((LEVELS, chunks + 1)),
            pltpu.SemaphoreType.DMA((LEVELS, chunks + 1)),
            pltpu.SemaphoreType.DMA((LEVELS, 2)),
            pltpu.SemaphoreType.DMA((LEVELS, 2)),
        ],
        compiler_params=pltpu.CompilerParams(
            collective_id=0, has_side_effects=True, vmem_limit_bytes=56 * 1024 * 1024),
    )(jnp.transpose(angle_offset, (1, 2, 0)), jnp.transpose(integer_distance_shifts, (1, 2, 0)), image, angle_fraction, subcell_distance_shares)


def solution(mesh):
    placed = (P(None, "sub", "rng"),) + (P(None, None, "sub"),) * 4
    return jax.shard_map(
        per_device, mesh=mesh, in_specs=placed, out_specs=P(None, "sub", "rng"), check_vma=False)
```
